32 devices in a mesh: row: 2 (over x), col: 4 (over y, core), layer: 4 (over z).
Axes of the slice: x: 2, y: 2, z: 4, core: 2. Of those that a mesh axis runs over, the one named last changes fastest.
Arguments:
- a_tiles: bfloat16 [2, 16, 128, 4096], P('row', ('col', 'layer')), may hold values from -0.4375 to 0.4375
- a_rows: int32 [2, 16, 128], P('row', ('col', 'layer')), may hold values from 0 to 31
- a_cols: int32 [2, 16, 128], P('row', ('col', 'layer')), may hold values from 0 to 3
- a_count: int32 [2, 16], P('row', ('col', 'layer')), may hold values from 16 to 128, as said below
- p_tiles: bfloat16 [4, 16, 4, 4096], P('row', ('col', 'layer')), may hold values from -0.375 to 0.375
- p_cols: int32 [4, 16, 4], P('row', ('col', 'layer')), may hold values from -1 to 1
Outputs:
- coarse: float32 [64, 192], replicated
The draws below stay inside these ranges and needn't reach their ends.
Inputs may be any that keep to these rules, and one draw needn't show every extreme that they name: `a_count`: some device uses all 128 slots and some device only 16 of them.
All inputs are finite; a program needn't handle non-finite values.
Results may differ from the reference program's by a relative error of at most 0.0037.
Values may be sent and summed in bfloat16 or wider, within the bound.
A program may use at most 64 MiB of HBM per device.

```python
import jax
import jax.numpy as jnp
from jax import lax

TILE = 64
NP = 4
PB = 1
KR = 2
SA = 128
NKG = 16
FR = 32
KC = 4
NF = 64
W = 2
N_ROW = 2


def draw_a_count(key, part):
    first_key, second_key, third_key = jax.random.split(key, 3)
    device_total = N_ROW * NKG
    light_counts = jax.random.randint(first_key, (device_total,), SA // 8, SA // 2 + 1)
    heavy_mask = jax.random.randint(second_key, (device_total,), 0, 16) == 0
    counts = jnp.where(heavy_mask, SA, light_counts)
    chosen_spots = jax.random.permutation(third_key, device_total)
    counts = counts.at[chosen_spots[0]].set(SA)
    counts = counts.at[chosen_spots[1]].set(SA // 8)
    return counts.reshape(N_ROW, NKG).astype(jnp.int32)


def draw_a_rows(key, part):
    near_key, far_key, pick_key, layer_key = jax.random.split(jax.random.fold_in(key, 71), 4)
    shape = (N_ROW, NKG, SA)
    near_offset = jax.random.randint(near_key, shape, -1, 2)
    far_group = jax.random.randint(far_key, shape, 0, NKG)
    pick_near = jax.random.randint(pick_key, shape, 0, 2) == 0
    own_group = jnp.arange(NKG, dtype=jnp.int32)[None, :, None]
    residue = jnp.where(pick_near, (own_group + near_offset + NKG) % NKG, far_group)
    row_layer = jax.random.randint(layer_key, shape, 0, KR)
    return (row_layer * NKG + residue).astype(jnp.int32)


def touch_ends(values, own_key, low, largest):
    spot = [jax.random.randint(jax.random.fold_in(own_key, axis), (), 0, length) for axis, length in enumerate(values.shape)]
    main_axis = values.shape.index(max(values.shape))
    beside = spot[:main_axis] + [(spot[main_axis] + 1) % values.shape[main_axis]] + spot[main_axis + 1:]
    return values.at[tuple(spot)].set(low).at[tuple(beside)].set(largest)


def levels(rng, dims, cuts, least, largest):
    def one(position, parts):
        heights = jax.random.uniform(jax.random.fold_in(jax.random.fold_in(rng, 6), position), (parts,), jnp.float32, least / len(cuts), largest / len(cuts))
        return jnp.repeat(jnp.exp(heights), dims[position] // parts).reshape((-1,) + (1,) * (len(dims) - position - 1))

    gain = one(*cuts[0])
    for cut in cuts[1:]:
        gain = gain * one(*cut)
    return gain


def gaussian(stream_key, shape, spread, bound, pieces=(), held_as=jnp.bfloat16):
    level = levels(stream_key, shape, pieces, -0.22, 0.18) if pieces else 1.0
    values = jax.random.normal(stream_key, shape, jnp.float32) * spread * level
    return jnp.minimum(jnp.maximum(values, -bound), bound).astype(held_as)


def setup_inputs(seed: int = 0) -> dict:
    key_list = jax.random.split(jax.random.key(seed), 7)
    return {
        "a_tiles": gaussian(key_list[0], (N_ROW, NKG, SA, TILE * TILE), (SA // KR * NF // 20) ** -0.5, 0.4375, ((0, 2), (1, 16))),
        "a_rows": draw_a_rows(jax.random.fold_in(key_list[6], 71), 0),
        "a_cols": touch_ends(jax.random.randint(key_list[2], (N_ROW, NKG, SA), 0, KC), jax.random.fold_in(key_list[2], 1), 0, KC - 1).astype(jnp.int32),
        "a_count": draw_a_count(jax.random.fold_in(key_list[6], 71), 0),
        "p_tiles": gaussian(key_list[4], (KC, NKG, NP, TILE * TILE), (TILE * NP) ** -0.5, 0.375, ((0, 2), (1, 16))),
        "p_cols": touch_ends(jax.random.randint(key_list[5], (KC, NKG, NP), -1, W), jax.random.fold_in(key_list[5], 1), -1, W - 1).astype(jnp.int32),
    }


def reference(a_tiles, a_rows, a_cols, a_count, p_tiles, p_cols):
    window_width = W * TILE
    onehot = (p_cols[..., None] == jnp.arange(W, dtype=jnp.int32)).astype(jnp.float32)
    tile_values = p_tiles.astype(jnp.float32).reshape(KC, NKG, NP, TILE, TILE)
    window = jnp.einsum('tfsj,tfsab->tfajb', onehot, tile_values)
    window = window.reshape(KC, NKG, TILE, window_width).astype(jnp.bfloat16)
    slot_ids = jnp.arange(SA, dtype=jnp.int32)

    def visit_device(running, device_inputs):
        device_index, tiles_dev, rows_dev, cols_dev, live_count = device_inputs
        row_group = device_index // NKG
        col_group = device_index % NKG
        picked = window[cols_dev, col_group].astype(jnp.float32)
        live_mask = (slot_ids < live_count).astype(jnp.float32)
        masked = tiles_dev.astype(jnp.float32).reshape(SA, TILE, TILE) * live_mask[:, None, None]
        products = jnp.einsum('sab,sbc->sac', masked, picked)
        row_block = jnp.zeros((FR, TILE, window_width), jnp.float32).at[rows_dev].add(products)
        first_row = (row_group * FR).astype(jnp.int32)
        current = lax.dynamic_slice_in_dim(running, first_row, FR, 0)
        running = lax.dynamic_update_slice_in_dim(running, current + row_block, first_row, 0)
        return running, None

    device_inputs = (
        jnp.arange(N_ROW * NKG, dtype=jnp.int32),
        a_tiles.reshape(N_ROW * NKG, SA, TILE * TILE),
        a_rows.reshape(N_ROW * NKG, SA),
        a_cols.reshape(N_ROW * NKG, SA),
        a_count.reshape(N_ROW * NKG),
    )
    product, _ = lax.scan(visit_device, jnp.zeros((NF, TILE, window_width), jnp.float32), device_inputs)
    prolong = window.reshape(NF * TILE, window_width).astype(jnp.float32)
    galerkin = jnp.dot(prolong.T, product.reshape(NF * TILE, window_width), precision=lax.Precision.HIGHEST)
    panel_size = PB * TILE
    return jnp.concatenate([galerkin[:panel_size, :panel_size], galerkin[:panel_size, panel_size:], galerkin[panel_size:, panel_size:]], axis=1)
```

```python
import functools
import math

import jax
import jax.numpy as jnp
from jax import lax
from jax.experimental import pallas as pl
from jax.experimental.pallas import tpu as pltpu
from jax.sharding import PartitionSpec as P

TILE = 64
PB = 1
LANES = 128
CHUNK = 8
MESH = pl.DeviceIdType.MESH


def kernel(
    sizes,
    a_hbm,
    rows_ref,
    cols_ref,
    count_ref,
    p_ref,
    pcols_ref,
    out_ref,
    a_ref,
    wf_ref,
    wb_ref,
    colw_ref,
    roww_ref,
    lhs_ref,
    rhs_ref,
    y_ref,
    y2_ref,
    part_ref,
    recv_ref,
    gath_ref,
    a_sem,
    colw_send,
    colw_recv,
    roww_send,
    roww_recv,
    part_send,
    part_recv,
    gath_send,
    gath_recv,
):
    row_devices, col_devices, layer_devices, step, inverse = sizes
    groups = col_devices * layer_devices
    total = row_devices * groups
    local_rows = p_ref.shape[0]
    slots_p = p_ref.shape[2]
    slot_total = a_ref.shape[0]
    pairs = TILE // 2
    block_rows = local_rows * groups
    block_cols = local_rows * row_devices
    chunks = part_ref.shape[0]

    my_row = lax.axis_index("row")
    my_group = lax.axis_index("col") * layer_devices + lax.axis_index("layer")
    me = my_row * groups + my_group

    def place(index):
        rest = lax.rem(index, groups)
        return (
            lax.div(index, groups),
            lax.div(rest, layer_devices),
            lax.rem(rest, layer_devices),
        )

    barrier = pltpu.get_barrier_semaphore()

    @pl.loop(1, total)
    def _(k):
        pl.semaphore_signal(
            barrier, inc=1, device_id=place(lax.rem(me + k, total)), device_id_type=MESH
        )

    a_copy = pltpu.make_async_copy(a_hbm.at[0, 0], a_ref, a_sem)
    a_copy.start()

    slot_ids = lax.broadcasted_iota(jnp.int32, (slots_p, 1), 0)
    for t in range(local_rows):
        tiles = p_ref[t, 0].astype(jnp.float32)
        ids = jnp.full((slots_p, 1), -1, jnp.int32)
        for s in range(slots_p):
            ids = jnp.where(slot_ids == s, pcols_ref[t, 0, s], ids)
        for panel in range(2):
            picked = jnp.sum(jnp.where(ids == panel, tiles, 0.0), axis=0, keepdims=True)
            for j in range(pairs):
                wf_ref[t, j : j + 1, panel * LANES : (panel + 1) * LANES] = picked[
                    :, j * LANES : (j + 1) * LANES
                ]
    own = wf_ref[...].astype(jnp.bfloat16)
    wb_ref[...] = own
    colw_ref[my_row] = own
    roww_ref[my_group] = own

    pl.semaphore_wait(barrier, total - 1)

    @pl.loop(1, row_devices)
    def _(k):
        peer = lax.rem(my_row + k, row_devices)
        pltpu.make_async_remote_copy(
            src_ref=wb_ref,
            dst_ref=colw_ref.at[my_row],
            send_sem=colw_send,
            recv_sem=colw_recv,
            device_id=place(peer * groups + my_group),
            device_id_type=MESH,
        ).start()

    @pl.loop(1, groups)
    def _(k):
        peer = lax.rem(my_group + k, groups)
        pltpu.make_async_remote_copy(
            src_ref=wb_ref,
            dst_ref=roww_ref.at[my_group],
            send_sem=roww_send,
            recv_sem=roww_recv,
            device_id=place(my_row * groups + peer),
            device_id_type=MESH,
        ).start()

    def wait_bytes(ref, sem):
        pltpu.make_async_copy(ref, ref, sem).wait()

    a_copy.wait()
    ids = cols_ref[0] * block_rows + rows_ref[0]
    slot_row = lax.broadcasted_iota(jnp.int32, (1, slot_total), 1)
    ids = jnp.where(slot_row < count_ref[0, 0], ids, -1)
    for c in range(block_cols):
        wanted = c * block_rows + lax.broadcasted_iota(
            jnp.int32, (block_rows, slot_total), 0
        )
        onehot = (ids == wanted).astype(jnp.float32).astype(jnp.bfloat16)
        dense = jnp.dot(onehot, a_ref[...], preferred_element_type=jnp.float32)
        dense = dense.astype(jnp.bfloat16)
        for j in range(pairs):
            lhs_ref[j * block_rows : (j + 1) * block_rows, c * LANES : (c + 1) * LANES] = (
                dense[:, j * LANES : (j + 1) * LANES]
            )

    wait_bytes(colw_ref.at[pl.ds(0, row_devices - 1)], colw_recv)
    out_row = lax.broadcasted_iota(jnp.int32, (LANES, TILE), 0)
    in_row = lax.broadcasted_iota(jnp.int32, (LANES, TILE), 1)
    parity = out_row // TILE
    inner = out_row % TILE
    spread = jnp.where((inner % 2) == parity, 0, pairs) + inner // 2
    spread = (in_row == spread).astype(jnp.float32).astype(jnp.bfloat16)
    lane = lax.broadcasted_iota(jnp.int32, (LANES, 2 * LANES), 1)
    sub = lax.broadcasted_iota(jnp.int32, (LANES, 2 * LANES), 0)
    keep = ((lane // TILE) % 2) == (sub // TILE)
    for c in range(block_cols):
        block = colw_ref[c // local_rows, c % local_rows].astype(jnp.float32)
        swapped = jnp.concatenate(
            [pltpu.roll(block[:, :LANES], TILE, 1), pltpu.roll(block[:, LANES:], TILE, 1)],
            axis=1,
        )
        both = jnp.concatenate([block, swapped], axis=0).astype(jnp.bfloat16)
        made = jnp.dot(spread, both, preferred_element_type=jnp.float32)
        rhs_ref[c * LANES : (c + 1) * LANES, :] = jnp.where(keep, made, 0.0).astype(
            jnp.bfloat16
        )

    y = jnp.dot(lhs_ref[...], rhs_ref[...], preferred_element_type=jnp.float32)
    for h in range(2):
        y_ref[h] = y[:, h * LANES : (h + 1) * LANES]
    for g in range(groups):
        for t in range(local_rows):
            at = (g * local_rows + t) * pairs
            for h in range(2):
                y2_ref[at : at + pairs, h * LANES : (h + 1) * LANES] = y_ref[
                    h, pl.ds(t * groups + g, pairs, stride=block_rows), :
                ].astype(jnp.bfloat16)

    wait_bytes(roww_ref.at[pl.ds(0, groups - 1)], roww_recv)
    window = roww_ref[...].reshape(block_rows * pairs, 2 * LANES)
    m = lax.dot_general(
        window,
        y2_ref[...],
        (((0,), (0,)), ((), ())),
        preferred_element_type=jnp.float32,
    )

    def fold(i, j):
        top = m[i * LANES : i * LANES + TILE, j * LANES : (j + 1) * LANES]
        low = m[i * LANES + TILE : (i + 1) * LANES, j * LANES : (j + 1) * LANES]
        return top + pltpu.roll(low, TILE, 1)

    left = lax.broadcasted_iota(jnp.int32, (TILE, LANES), 1) < TILE
    upper = jnp.where(left, fold(0, 0), pltpu.roll(fold(0, 1), TILE, 1))
    corner = fold(1, 1)
    lower = jnp.where(
        left[: TILE // 2], corner[: TILE // 2], pltpu.roll(corner[TILE // 2 :], TILE, 1)
    )
    part_ref[...] = jnp.concatenate([upper, lower], axis=0).reshape(chunks, CHUNK, LANES)

    my_chunk = lax.rem(me * inverse, total)

    @pl.loop(0, chunks)
    def _(o):
        owner = lax.rem(o * step, total)

        @pl.when(owner != me)
        def _():
            pltpu.make_async_remote_copy(
                src_ref=part_ref.at[o],
                dst_ref=recv_ref.at[me],
                send_sem=part_send,
                recv_sem=part_recv,
                device_id=place(owner),
                device_id_type=MESH,
            ).start()

    @pl.when(my_chunk < chunks)
    def _():
        recv_ref[me] = part_ref[my_chunk]
        wait_bytes(recv_ref.at[pl.ds(0, total - 1)], part_recv)
        gath_ref[my_chunk] = jnp.sum(recv_ref[...], axis=0)

        @pl.loop(1, total)
        def _(k):
            pltpu.make_async_remote_copy(
                src_ref=gath_ref.at[my_chunk],
                dst_ref=gath_ref.at[my_chunk],
                send_sem=gath_send,
                recv_sem=gath_recv,
                device_id=place(lax.rem(me + k, total)),
                device_id_type=MESH,
            ).start()

        wait_bytes(gath_ref.at[pl.ds(0, chunks - 1)], gath_recv)
        wait_bytes(part_ref.at[pl.ds(0, chunks - 1)], part_send)
        wait_bytes(recv_ref.at[pl.ds(0, total - 1)], gath_send)

    @pl.when(my_chunk >= chunks)
    def _():
        wait_bytes(gath_ref, gath_recv)
        wait_bytes(part_ref, part_send)

    half = TILE // CHUNK
    out_ref[:, :LANES] = gath_ref[:half].reshape(TILE, LANES)
    corner = gath_ref[half:].reshape(TILE // 2, LANES)
    out_ref[: TILE // 2, LANES:] = corner[:, :TILE]
    out_ref[TILE // 2 :, LANES:] = pltpu.roll(corner, TILE, 1)[:, :TILE]
    wait_bytes(colw_ref.at[pl.ds(0, row_devices - 1)], colw_send)
    wait_bytes(roww_ref.at[pl.ds(0, groups - 1)], roww_send)


def per_device(a_tiles, a_rows, a_cols, a_count, p_tiles, p_cols):
    row_devices = lax.axis_size("row")
    col_devices = lax.axis_size("col")
    layer_devices = lax.axis_size("layer")
    groups = col_devices * layer_devices
    total = row_devices * groups
    local_rows = p_tiles.shape[0]
    slot_total = a_tiles.shape[2]
    pairs = TILE // 2
    block_rows = local_rows * groups
    block_cols = local_rows * row_devices
    chunks = (TILE + TILE // 2) // CHUNK
    step = next(s for s in range(5, total + 5) if math.gcd(s, total) == 1)
    inverse = pow(step, -1, total)
    sizes = (row_devices, col_devices, layer_devices, step, inverse)
    vmem = pl.BlockSpec(memory_space=pltpu.VMEM)
    smem = pl.BlockSpec(memory_space=pltpu.SMEM)
    wide = 2 * LANES
    return pl.pallas_call(
        functools.partial(kernel, sizes),
        out_shape=jax.ShapeDtypeStruct((PB * TILE, 3 * PB * TILE), jnp.float32),
        in_specs=[pl.BlockSpec(memory_space=pl.ANY), vmem, vmem, smem, vmem, smem],
        out_specs=vmem,
        scratch_shapes=[
            pltpu.VMEM((slot_total, TILE * TILE), jnp.bfloat16),
            pltpu.VMEM((local_rows, pairs, wide), jnp.float32),
            pltpu.VMEM((local_rows, pairs, wide), jnp.bfloat16),
            pltpu.VMEM((row_devices, local_rows, pairs, wide), jnp.bfloat16),
            pltpu.VMEM((groups, local_rows, pairs, wide), jnp.bfloat16),
            pltpu.VMEM((pairs * block_rows, block_cols * LANES), jnp.bfloat16),
            pltpu.VMEM((block_cols * LANES, wide), jnp.bfloat16),
            pltpu.VMEM((2, pairs * block_rows, LANES), jnp.float32),
            pltpu.VMEM((pairs * block_rows, wide), jnp.bfloat16),
            pltpu.VMEM((chunks, CHUNK, LANES), jnp.float32),
            pltpu.VMEM((total, CHUNK, LANES), jnp.float32),
            pltpu.VMEM((chunks, CHUNK, LANES), jnp.float32),
        ]
        + [pltpu.SemaphoreType.DMA] * 9,
        compiler_params=pltpu.CompilerParams(
            collective_id=0, has_side_effects=True, vmem_limit_bytes=56 << 20
        ),
    )(a_tiles, a_rows, a_cols, a_count, p_tiles, p_cols)


def solution(mesh):
    placed = (
        P("row", ("col", "layer"), None, None),
        P("row", ("col", "layer"), None),
        P("row", ("col", "layer"), None),
        P("row", ("col", "layer")),
        P("row", ("col", "layer"), None, None),
        P("row", ("col", "layer"), None),
    )
    return jax.shard_map(per_device, mesh=mesh, in_specs=placed, out_specs=P(), check_vma=False)
```

```python
import functools

import jax
import jax.numpy as jnp
from jax import lax
from jax.experimental import pallas as pl
from jax.experimental.pallas import tpu as pltpu
from jax.sharding import PartitionSpec as P

TILE = 64
PB = 1
LANES = 128
CHUNK = 8
MESH = pl.DeviceIdType.MESH


def kernel(
    sizes,
    a_hbm,
    rows_ref,
    cols_ref,
    count_ref,
    p_ref,
    pcols_ref,
    out_ref,
    a_ref,
    wf_ref,
    wb_ref,
    colw_ref,
    roww_ref,
    lhs_ref,
    rhs_ref,
    y_ref,
    y2_ref,
    yrecv_ref,
    ysum_ref,
    part_ref,
    first_ref,
    second_ref,
    third_ref,
    a_sem,
    colw_send,
    colw_recv,
    roww_send,
    roww_recv,
    pair_send,
    pair_recv,
    first_send,
    first_recv,
    second_send,
    second_recv,
    third_send,
    third_recv,
):
    row_devices, col_devices, layer_devices = sizes
    groups = col_devices * layer_devices
    quads = 2 * row_devices
    spots = groups // 2
    local_rows = p_ref.shape[0]
    slots_p = p_ref.shape[2]
    slot_total = a_ref.shape[0]
    pairs = TILE // 2
    block_rows = local_rows * groups
    block_cols = local_rows * row_devices
    my_row = lax.axis_index("row")
    my_col = lax.axis_index("col")
    my_layer = lax.axis_index("layer")
    my_pair = lax.rem(my_col, 2)
    my_quad = my_row * 2 + my_pair
    my_spot = lax.div(my_col, 2) * layer_devices + my_layer

    def place(quad, spot):
        return (
            lax.div(quad, 2),
            lax.div(spot, layer_devices) * 2 + lax.rem(quad, 2),
            lax.rem(spot, layer_devices),
        )

    def around(mine, count, act):
        if count <= 8:
            for k in range(1, count):
                act(lax.rem(mine + k, count))
        else:

            @pl.loop(1, count)
            def _(k):
                act(lax.rem(mine + k, count))

    def send(src, dst, send_sem, recv_sem, device):
        pltpu.make_async_remote_copy(
            src_ref=src,
            dst_ref=dst,
            send_sem=send_sem,
            recv_sem=recv_sem,
            device_id=device,
            device_id_type=MESH,
        ).start()

    def wait_bytes(ref, sem):
        pltpu.make_async_copy(ref, ref, sem).wait()

    barrier = pltpu.get_barrier_semaphore()

    def greet(device):
        pl.semaphore_signal(barrier, inc=1, device_id=device, device_id_type=MESH)

    around(my_spot, spots, lambda peer: greet(place(my_quad, peer)))
    around(my_quad, quads, lambda peer: greet(place(peer, my_spot)))

    a_copy = pltpu.make_async_copy(a_hbm.at[0, 0], a_ref, a_sem)
    a_copy.start()

    slot_ids = lax.broadcasted_iota(jnp.int32, (slots_p, 1), 0)
    for t in range(local_rows):
        tiles = p_ref[t, 0].astype(jnp.float32)
        ids = jnp.full((slots_p, 1), -1, jnp.int32)
        for s in range(slots_p):
            ids = jnp.where(slot_ids == s, pcols_ref[t, 0, s], ids)
        for panel in range(2):
            picked = jnp.sum(jnp.where(ids == panel, tiles, 0.0), axis=0, keepdims=True)
            for j in range(pairs):
                wf_ref[t, j : j + 1, panel * LANES : (panel + 1) * LANES] = picked[
                    :, j * LANES : (j + 1) * LANES
                ]
    own = wf_ref[...].astype(jnp.bfloat16)
    wb_ref[...] = own
    colw_ref[my_row] = own
    roww_ref[my_spot] = own

    pl.semaphore_wait(barrier, spots + quads - 2)
    around(
        my_row,
        row_devices,
        lambda peer: send(
            wb_ref,
            colw_ref.at[my_row],
            colw_send,
            colw_recv,
            place(peer * 2 + my_pair, my_spot),
        ),
    )
    around(
        my_spot,
        spots,
        lambda peer: send(
            wb_ref, roww_ref.at[my_spot], roww_send, roww_recv, place(my_quad, peer)
        ),
    )

    a_copy.wait()
    ids = cols_ref[0] * block_rows + rows_ref[0]
    slot_row = lax.broadcasted_iota(jnp.int32, (1, slot_total), 1)
    ids = jnp.where(slot_row < count_ref[0, 0], ids, -1)
    for c in range(block_cols):
        wanted = c * block_rows + lax.broadcasted_iota(
            jnp.int32, (block_rows, slot_total), 0
        )
        onehot = (ids == wanted).astype(jnp.float32).astype(jnp.bfloat16)
        dense = jnp.dot(onehot, a_ref[...], preferred_element_type=jnp.float32)
        dense = dense.astype(jnp.bfloat16)
        for j in range(pairs):
            lhs_ref[j * block_rows : (j + 1) * block_rows, c * LANES : (c + 1) * LANES] = (
                dense[:, j * LANES : (j + 1) * LANES]
            )

    wait_bytes(colw_ref.at[pl.ds(0, row_devices - 1)], colw_recv)
    out_row = lax.broadcasted_iota(jnp.int32, (LANES, TILE), 0)
    in_row = lax.broadcasted_iota(jnp.int32, (LANES, TILE), 1)
    parity = out_row // TILE
    inner = out_row % TILE
    spread = jnp.where((inner % 2) == parity, 0, pairs) + inner // 2
    spread = (in_row == spread).astype(jnp.float32).astype(jnp.bfloat16)
    lane = lax.broadcasted_iota(jnp.int32, (LANES, 2 * LANES), 1)
    sub = lax.broadcasted_iota(jnp.int32, (LANES, 2 * LANES), 0)
    keep = ((lane // TILE) % 2) == (sub // TILE)
    for c in range(block_cols):
        block = colw_ref[c // local_rows, c % local_rows].astype(jnp.float32)
        swapped = jnp.concatenate(
            [pltpu.roll(block[:, :LANES], TILE, 1), pltpu.roll(block[:, LANES:], TILE, 1)],
            axis=1,
        )
        both = jnp.concatenate([block, swapped], axis=0).astype(jnp.bfloat16)
        made = jnp.dot(spread, both, preferred_element_type=jnp.float32)
        rhs_ref[c * LANES : (c + 1) * LANES, :] = jnp.where(keep, made, 0.0).astype(
            jnp.bfloat16
        )

    y = jnp.dot(lhs_ref[...], rhs_ref[...], preferred_element_type=jnp.float32)
    for h in range(2):
        y_ref[h] = y[:, h * LANES : (h + 1) * LANES]
    def product_rows(pair, spot, t):
        group = (lax.div(spot, layer_devices) * 2 + pair) * layer_devices + lax.rem(
            spot, layer_devices
        )
        return [
            y_ref[h, pl.ds(t * groups + group, pairs, stride=block_rows), :]
            for h in range(2)
        ]

    for spot in range(spots):
        for t in range(local_rows):
            at = (spot * local_rows + t) * pairs
            for h, rows in enumerate(product_rows(1 - my_pair, spot, t)):
                y2_ref[at : at + pairs, h * LANES : (h + 1) * LANES] = rows.astype(
                    jnp.bfloat16
                )
    sibling = place(my_row * 2 + 1 - my_pair, my_spot)
    send(y2_ref, yrecv_ref, pair_send, pair_recv, sibling)
    wait_bytes(yrecv_ref, pair_recv)
    for spot in range(spots):
        for t in range(local_rows):
            at = (spot * local_rows + t) * pairs
            for h, rows in enumerate(product_rows(my_pair, spot, t)):
                spans = (slice(at, at + pairs), slice(h * LANES, (h + 1) * LANES))
                ysum_ref[spans] = (rows + yrecv_ref[spans].astype(jnp.float32)).astype(
                    jnp.bfloat16
                )

    wait_bytes(roww_ref.at[pl.ds(0, spots - 1)], roww_recv)
    window = roww_ref[...].reshape(spots * local_rows * pairs, 2 * LANES)
    m = lax.dot_general(
        window,
        ysum_ref[...],
        (((0,), (0,)), ((), ())),
        preferred_element_type=jnp.float32,
    )

    def fold(i, j):
        top = m[i * LANES : i * LANES + TILE, j * LANES : (j + 1) * LANES]
        low = m[i * LANES + TILE : (i + 1) * LANES, j * LANES : (j + 1) * LANES]
        return top + pltpu.roll(low, TILE, 1)

    left = lax.broadcasted_iota(jnp.int32, (TILE, LANES), 1) < TILE
    upper = jnp.where(left, fold(0, 0), pltpu.roll(fold(0, 1), TILE, 1))
    corner = fold(1, 1)
    lower = jnp.where(
        left[: TILE // 2], corner[: TILE // 2], pltpu.roll(corner[TILE // 2 :], TILE, 1)
    )
    packed = [upper, lower]
    spare = part_ref.shape[0] * part_ref.shape[1] - TILE - TILE // 2
    if spare:
        packed.append(jnp.zeros((spare, LANES), jnp.float32))
    part_ref[...] = jnp.concatenate(packed, axis=0).reshape(part_ref.shape)

    around(
        my_quad,
        quads,
        lambda peer: send(
            part_ref.at[peer],
            first_ref.at[my_quad],
            first_send,
            first_recv,
            place(peer, my_spot),
        ),
    )
    first_ref[my_quad] = part_ref[my_quad]
    wait_bytes(first_ref.at[pl.ds(0, quads - 1)], first_recv)
    second_ref[my_spot] = jnp.sum(first_ref[...], axis=0)
    around(
        my_spot,
        spots,
        lambda peer: send(
            second_ref.at[my_spot],
            second_ref.at[my_spot],
            second_send,
            second_recv,
            place(my_quad, peer),
        ),
    )
    wait_bytes(second_ref.at[pl.ds(0, spots - 1)], second_recv)
    third_ref[my_quad] = jnp.sum(second_ref[...], axis=0)
    around(
        my_quad,
        quads,
        lambda peer: send(
            third_ref.at[my_quad],
            third_ref.at[my_quad],
            third_send,
            third_recv,
            place(peer, my_spot),
        ),
    )
    wait_bytes(third_ref.at[pl.ds(0, quads - 1)], third_recv)

    summed = third_ref[...].reshape(-1, LANES)
    out_ref[:, :LANES] = summed[:TILE]
    corner = summed[TILE : TILE + TILE // 2]
    out_ref[: TILE // 2, LANES:] = corner[:, :TILE]
    out_ref[TILE // 2 :, LANES:] = pltpu.roll(corner, TILE, 1)[:, :TILE]
    wait_bytes(colw_ref.at[pl.ds(0, row_devices - 1)], colw_send)
    wait_bytes(roww_ref.at[pl.ds(0, spots - 1)], roww_send)
    wait_bytes(y2_ref, pair_send)
    wait_bytes(first_ref.at[pl.ds(0, quads - 1)], first_send)
    wait_bytes(second_ref.at[pl.ds(0, spots - 1)], second_send)
    wait_bytes(third_ref.at[pl.ds(0, quads - 1)], third_send)


def per_device(a_tiles, a_rows, a_cols, a_count, p_tiles, p_cols):
    row_devices = lax.axis_size("row")
    col_devices = lax.axis_size("col")
    layer_devices = lax.axis_size("layer")
    groups = col_devices * layer_devices
    spots = groups // 2
    quads = 2 * row_devices
    local_rows = p_tiles.shape[0]
    slot_total = a_tiles.shape[2]
    pairs = TILE // 2
    block_rows = local_rows * groups
    block_cols = local_rows * row_devices
    packed_rows = TILE + TILE // 2
    chunk = pl.cdiv(pl.cdiv(packed_rows, quads), CHUNK) * CHUNK
    half_rows = spots * local_rows * pairs
    sizes = (row_devices, col_devices, layer_devices)
    vmem = pl.BlockSpec(memory_space=pltpu.VMEM)
    smem = pl.BlockSpec(memory_space=pltpu.SMEM)
    wide = 2 * LANES
    return pl.pallas_call(
        functools.partial(kernel, sizes),
        out_shape=jax.ShapeDtypeStruct((PB * TILE, 3 * PB * TILE), jnp.float32),
        in_specs=[pl.BlockSpec(memory_space=pl.ANY), vmem, vmem, smem, vmem, smem],
        out_specs=vmem,
        scratch_shapes=[
            pltpu.VMEM((slot_total, TILE * TILE), jnp.bfloat16),
            pltpu.VMEM((local_rows, pairs, wide), jnp.float32),
            pltpu.VMEM((local_rows, pairs, wide), jnp.bfloat16),
            pltpu.VMEM((row_devices, local_rows, pairs, wide), jnp.bfloat16),
            pltpu.VMEM((spots, local_rows, pairs, wide), jnp.bfloat16),
            pltpu.VMEM((pairs * block_rows, block_cols * LANES), jnp.bfloat16),
            pltpu.VMEM((block_cols * LANES, wide), jnp.bfloat16),
            pltpu.VMEM((2, pairs * block_rows, LANES), jnp.float32),
            pltpu.VMEM((half_rows, wide), jnp.bfloat16),
            pltpu.VMEM((half_rows, wide), jnp.bfloat16),
            pltpu.VMEM((half_rows, wide), jnp.bfloat16),
            pltpu.VMEM((quads, chunk, LANES), jnp.float32),
            pltpu.VMEM((quads, chunk, LANES), jnp.float32),
            pltpu.VMEM((spots, chunk, LANES), jnp.float32),
            pltpu.VMEM((quads, chunk, LANES), jnp.float32),
        ]
        + [pltpu.SemaphoreType.DMA] * 13,
        compiler_params=pltpu.CompilerParams(
            collective_id=0, has_side_effects=True, vmem_limit_bytes=56 << 20
        ),
    )(a_tiles, a_rows, a_cols, a_count, p_tiles, p_cols)


def solution(mesh):
    placed = (
        P("row", ("col", "layer"), None, None),
        P("row", ("col", "layer"), None),
        P("row", ("col", "layer"), None),
        P("row", ("col", "layer")),
        P("row", ("col", "layer"), None, None),
        P("row", ("col", "layer"), None),
    )
    return jax.shard_map(per_device, mesh=mesh, in_specs=placed, out_specs=P(), check_vma=False)
```

```python
import functools

import jax
import jax.numpy as jnp
from jax import lax
from jax.experimental import pallas as pl
from jax.experimental.pallas import tpu as pltpu
from jax.sharding import PartitionSpec as P

TILE = 64
PB = 1
LANES = 128
CHUNK = 8
MESH = pl.DeviceIdType.MESH


def kernel(
    sizes,
    a_hbm,
    rows_ref,
    cols_ref,
    count_ref,
    p_ref,
    pcols_ref,
    out_ref,
    a_ref,
    wf_ref,
    wb_ref,
    colw_ref,
    roww_ref,
    lhs_ref,
    rhs_ref,
    y_ref,
    y2_ref,
    yrecv_ref,
    ysum_ref,
    part_ref,
    first_ref,
    second_ref,
    third_ref,
    a_sem,
    colw_send,
    colw_recv,
    roww_send,
    roww_recv,
    pair_send,
    pair_recv,
    first_send,
    first_recv,
    second_send,
    second_recv,
    third_send,
    third_recv,
):
    row_devices, col_devices, layer_devices = sizes
    groups = col_devices * layer_devices
    quads = 2 * row_devices
    spots = groups // 2
    local_rows = p_ref.shape[0]
    slots_p = p_ref.shape[2]
    slot_total = a_ref.shape[0]
    pairs = TILE // 2
    block_rows = local_rows * groups
    block_cols = local_rows * row_devices
    my_row = lax.axis_index("row")
    my_col = lax.axis_index("col")
    my_layer = lax.axis_index("layer")
    my_pair = lax.rem(my_col, 2)
    my_quad = my_row * 2 + my_pair
    my_spot = lax.div(my_col, 2) * layer_devices + my_layer

    def place(quad, spot):
        return (
            lax.div(quad, 2),
            lax.div(spot, layer_devices) * 2 + lax.rem(quad, 2),
            lax.rem(spot, layer_devices),
        )

    def around(mine, count, act):
        if count <= 8:
            for k in range(1, count):
                act(lax.rem(mine + k, count))
        else:

            @pl.loop(1, count)
            def _(k):
                act(lax.rem(mine + k, count))

    def send(src, dst, send_sem, recv_sem, device):
        pltpu.make_async_remote_copy(
            src_ref=src,
            dst_ref=dst,
            send_sem=send_sem,
            recv_sem=recv_sem,
            device_id=device,
            device_id_type=MESH,
        ).start()

    def wait_bytes(ref, sem):
        pltpu.make_async_copy(ref, ref, sem).wait()

    barrier = pltpu.get_barrier_semaphore()

    def greet(device):
        pl.semaphore_signal(barrier, inc=1, device_id=device, device_id_type=MESH)

    around(my_spot, spots, lambda peer: greet(place(my_quad, peer)))
    around(my_quad, quads, lambda peer: greet(place(peer, my_spot)))

    a_copy = pltpu.make_async_copy(a_hbm.at[0, 0], a_ref, a_sem)
    a_copy.start()

    slot_ids = lax.broadcasted_iota(jnp.int32, (slots_p, 1), 0)
    for t in range(local_rows):
        tiles = p_ref[t, 0].astype(jnp.float32)
        ids = jnp.full((slots_p, 1), -1, jnp.int32)
        for s in range(slots_p):
            ids = jnp.where(slot_ids == s, pcols_ref[t, 0, s], ids)
        for panel in range(2):
            picked = jnp.sum(jnp.where(ids == panel, tiles, 0.0), axis=0, keepdims=True)
            for j in range(pairs):
                wf_ref[t, j : j + 1, panel * LANES : (panel + 1) * LANES] = picked[
                    :, j * LANES : (j + 1) * LANES
                ]
    own = wf_ref[...].astype(jnp.bfloat16)
    wb_ref[...] = own
    colw_ref[my_row] = own
    roww_ref[my_spot] = own

    pl.semaphore_wait(barrier, spots + quads - 2)
    around(
        my_row,
        row_devices,
        lambda peer: send(
            wb_ref,
            colw_ref.at[my_row],
            colw_send,
            colw_recv,
            place(peer * 2 + my_pair, my_spot),
        ),
    )
    around(
        my_spot,
        spots,
        lambda peer: send(
            wb_ref, roww_ref.at[my_spot], roww_send, roww_recv, place(my_quad, peer)
        ),
    )

    a_copy.wait()
    ids = cols_ref[0] * block_rows + rows_ref[0]
    slot_row = lax.broadcasted_iota(jnp.int32, (1, slot_total), 1)
    ids = jnp.where(slot_row < count_ref[0, 0], ids, -1)
    for c in range(block_cols):
        wanted = c * block_rows + lax.broadcasted_iota(
            jnp.int32, (block_rows, slot_total), 0
        )
        onehot = (ids == wanted).astype(jnp.float32).astype(jnp.bfloat16)
        dense = jnp.dot(onehot, a_ref[...], preferred_element_type=jnp.float32)
        dense = dense.astype(jnp.bfloat16)
        for j in range(pairs):
            lhs_ref[j * block_rows : (j + 1) * block_rows, c * LANES : (c + 1) * LANES] = (
                dense[:, j * LANES : (j + 1) * LANES]
            )

    wait_bytes(colw_ref.at[pl.ds(0, row_devices - 1)], colw_recv)
    out_row = lax.broadcasted_iota(jnp.int32, (LANES, TILE), 0)
    in_row = lax.broadcasted_iota(jnp.int32, (LANES, TILE), 1)
    parity = out_row // TILE
    inner = out_row % TILE
    spread = jnp.where((inner % 2) == parity, 0, pairs) + inner // 2
    spread = (in_row == spread).astype(jnp.float32).astype(jnp.bfloat16)
    lane = lax.broadcasted_iota(jnp.int32, (LANES, 2 * LANES), 1)
    sub = lax.broadcasted_iota(jnp.int32, (LANES, 2 * LANES), 0)
    keep = ((lane // TILE) % 2) == (sub // TILE)
    for c in range(block_cols):
        block = colw_ref[c // local_rows, c % local_rows].astype(jnp.float32)
        swapped = jnp.concatenate(
            [pltpu.roll(block[:, :LANES], TILE, 1), pltpu.roll(block[:, LANES:], TILE, 1)],
            axis=1,
        )
        both = jnp.concatenate([block, swapped], axis=0).astype(jnp.bfloat16)
        made = jnp.dot(spread, both, preferred_element_type=jnp.float32)
        rhs_ref[c * LANES : (c + 1) * LANES, :] = jnp.where(keep, made, 0.0).astype(
            jnp.bfloat16
        )

    y = jnp.dot(lhs_ref[...], rhs_ref[...], preferred_element_type=jnp.float32)
    for h in range(2):
        y_ref[h] = y[:, h * LANES : (h + 1) * LANES]
    def product_rows(pair, spot, t):
        group = (lax.div(spot, layer_devices) * 2 + pair) * layer_devices + lax.rem(
            spot, layer_devices
        )
        return [
            y_ref[h, pl.ds(t * groups + group, pairs, stride=block_rows), :]
            for h in range(2)
        ]

    for spot in range(spots):
        for t in range(local_rows):
            at = (spot * local_rows + t) * pairs
            for h, rows in enumerate(product_rows(1 - my_pair, spot, t)):
                y2_ref[at : at + pairs, h * LANES : (h + 1) * LANES] = rows.astype(
                    jnp.bfloat16
                )
    sibling = place(my_row * 2 + 1 - my_pair, my_spot)
    send(y2_ref, yrecv_ref, pair_send, pair_recv, sibling)
    wait_bytes(yrecv_ref, pair_recv)
    for spot in range(spots):
        for t in range(local_rows):
            at = (spot * local_rows + t) * pairs
            for h, rows in enumerate(product_rows(my_pair, spot, t)):
                spans = (slice(at, at + pairs), slice(h * LANES, (h + 1) * LANES))
                ysum_ref[spans] = (rows + yrecv_ref[spans].astype(jnp.float32)).astype(
                    jnp.bfloat16
                )

    wait_bytes(roww_ref.at[pl.ds(0, spots - 1)], roww_recv)
    window = roww_ref[...].reshape(spots * local_rows * pairs, 2 * LANES)
    m = lax.dot_general(
        window,
        ysum_ref[...],
        (((0,), (0,)), ((), ())),
        preferred_element_type=jnp.float32,
    )

    def fold(i, j):
        top = m[i * LANES : i * LANES + TILE, j * LANES : (j + 1) * LANES]
        low = m[i * LANES + TILE : (i + 1) * LANES, j * LANES : (j + 1) * LANES]
        return top + pltpu.roll(low, TILE, 1)

    left = lax.broadcasted_iota(jnp.int32, (TILE, LANES), 1) < TILE
    upper = jnp.where(left, fold(0, 0), pltpu.roll(fold(0, 1), TILE, 1))
    corner = fold(1, 1)
    lower = jnp.where(
        left[: TILE // 2], corner[: TILE // 2], pltpu.roll(corner[TILE // 2 :], TILE, 1)
    )
    packed = [upper, lower]
    spare = part_ref.shape[0] * part_ref.shape[1] - TILE - TILE // 2
    if spare:
        packed.append(jnp.zeros((spare, LANES), jnp.float32))
    part_ref[...] = jnp.concatenate(packed, axis=0).reshape(part_ref.shape)

    around(
        my_quad,
        quads,
        lambda peer: send(
            part_ref.at[peer],
            first_ref.at[my_quad],
            first_send,
            first_recv,
            place(peer, my_spot),
        ),
    )
    first_ref[my_quad] = part_ref[my_quad]
    wait_bytes(first_ref.at[pl.ds(0, quads - 1)], first_recv)
    second_ref[my_spot] = jnp.sum(first_ref[...], axis=0)
    around(
        my_spot,
        spots,
        lambda peer: send(
            second_ref.at[my_spot],
            second_ref.at[my_spot],
            second_send,
            second_recv,
            place(my_quad, peer),
        ),
    )
    wait_bytes(second_ref.at[pl.ds(0, spots - 1)], second_recv)
    third_ref[my_quad] = jnp.sum(second_ref[...], axis=0)
    around(
        my_quad,
        quads,
        lambda peer: send(
            third_ref.at[my_quad],
            third_ref.at[my_quad],
            third_send,
            third_recv,
            place(peer, my_spot),
        ),
    )
    wait_bytes(third_ref.at[pl.ds(0, quads - 1)], third_recv)

    summed = third_ref[...].reshape(-1, LANES)
    out_ref[:, :LANES] = summed[:TILE]
    corner = summed[TILE : TILE + TILE // 2]
    out_ref[: TILE // 2, LANES:] = corner[:, :TILE]
    out_ref[TILE // 2 :, LANES:] = pltpu.roll(corner, TILE, 1)[:, :TILE]
    wait_bytes(colw_ref.at[pl.ds(0, row_devices - 1)], colw_send)
    wait_bytes(roww_ref.at[pl.ds(0, spots - 1)], roww_send)
    wait_bytes(y2_ref, pair_send)
    wait_bytes(first_ref.at[pl.ds(0, quads - 1)], first_send)
    wait_bytes(second_ref.at[pl.ds(0, spots - 1)], second_send)
    wait_bytes(third_ref.at[pl.ds(0, quads - 1)], third_send)


def per_device(a_tiles, a_rows, a_cols, a_count, p_tiles, p_cols):
    row_devices = lax.axis_size("row")
    col_devices = lax.axis_size("col")
    layer_devices = lax.axis_size("layer")
    groups = col_devices * layer_devices
    spots = groups // 2
    quads = 2 * row_devices
    local_rows = p_tiles.shape[0]
    slot_total = a_tiles.shape[2]
    pairs = TILE // 2
    block_rows = local_rows * groups
    block_cols = local_rows * row_devices
    packed_rows = TILE + TILE // 2
    chunk = pl.cdiv(pl.cdiv(packed_rows, quads), CHUNK) * CHUNK
    half_rows = spots * local_rows * pairs
    sizes = (row_devices, col_devices, layer_devices)
    vmem = pl.BlockSpec(memory_space=pltpu.VMEM)
    smem = pl.BlockSpec(memory_space=pltpu.SMEM)
    wide = 2 * LANES
    return pl.pallas_call(
        functools.partial(kernel, sizes),
        out_shape=pltpu.VMEM((PB * TILE, 3 * PB * TILE), jnp.float32),
        in_specs=[pl.BlockSpec(memory_space=pl.ANY), vmem, vmem, smem, vmem, smem],
        out_specs=vmem,
        scratch_shapes=[
            pltpu.VMEM((slot_total, TILE * TILE), jnp.bfloat16),
            pltpu.VMEM((local_rows, pairs, wide), jnp.float32),
            pltpu.VMEM((local_rows, pairs, wide), jnp.bfloat16),
            pltpu.VMEM((row_devices, local_rows, pairs, wide), jnp.bfloat16),
            pltpu.VMEM((spots, local_rows, pairs, wide), jnp.bfloat16),
            pltpu.VMEM((pairs * block_rows, block_cols * LANES), jnp.bfloat16),
            pltpu.VMEM((block_cols * LANES, wide), jnp.bfloat16),
            pltpu.VMEM((2, pairs * block_rows, LANES), jnp.float32),
            pltpu.VMEM((half_rows, wide), jnp.bfloat16),
            pltpu.VMEM((half_rows, wide), jnp.bfloat16),
            pltpu.VMEM((half_rows, wide), jnp.bfloat16),
            pltpu.VMEM((quads, chunk, LANES), jnp.float32),
            pltpu.VMEM((quads, chunk, LANES), jnp.float32),
            pltpu.VMEM((spots, chunk, LANES), jnp.float32),
            pltpu.VMEM((quads, chunk, LANES), jnp.float32),
        ]
        + [pltpu.SemaphoreType.DMA] * 13,
        compiler_params=pltpu.CompilerParams(
            collective_id=0, has_side_effects=True, vmem_limit_bytes=56 << 20
        ),
    )(a_tiles, a_rows, a_cols, a_count, p_tiles, p_cols)


def solution(mesh):
    placed = (
        P("row", ("col", "layer"), None, None),
        P("row", ("col", "layer"), None),
        P("row", ("col", "layer"), None),
        P("row", ("col", "layer")),
        P("row", ("col", "layer"), None, None),
        P("row", ("col", "layer"), None),
    )
    return jax.shard_map(per_device, mesh=mesh, in_specs=placed, out_specs=P(), check_vma=False)
```

```python
import functools

import jax
import jax.numpy as jnp
from jax import lax
from jax.experimental import pallas as pl
from jax.experimental.pallas import tpu as pltpu
from jax.sharding import PartitionSpec as P

TILE = 64
PB = 1
LANES = 128
CHUNK = 8
MESH = pl.DeviceIdType.MESH


def kernel(
    sizes,
    a_hbm,
    rows_ref,
    cols_ref,
    count_ref,
    p_ref,
    pcols_ref,
    out_ref,
    a_ref,
    wf_ref,
    wb_ref,
    colw_ref,
    roww_ref,
    lhs_ref,
    rhs_ref,
    y_ref,
    y2_ref,
    yrecv_ref,
    ysum_ref,
    part_ref,
    first_ref,
    second_ref,
    third_ref,
    a_sem,
    colw_send,
    colw_recv,
    roww_send,
    roww_recv,
    pair_send,
    pair_recv,
    first_send,
    first_recv,
    second_send,
    second_recv,
    third_send,
    third_recv,
):
    row_devices, col_devices, layer_devices = sizes
    groups = col_devices * layer_devices
    quads = 2 * row_devices
    spots = groups // 2
    local_rows = p_ref.shape[0]
    slots_p = p_ref.shape[2]
    slot_total = a_ref.shape[0]
    pairs = TILE // 2
    block_rows = local_rows * groups
    block_cols = local_rows * row_devices
    my_row = lax.axis_index("row")
    my_col = lax.axis_index("col")
    my_layer = lax.axis_index("layer")
    my_pair = lax.rem(my_col, 2)
    my_quad = my_row * 2 + my_pair
    my_spot = lax.div(my_col, 2) * layer_devices + my_layer

    def place(quad, spot):
        return (
            lax.div(quad, 2),
            lax.div(spot, layer_devices) * 2 + lax.rem(quad, 2),
            lax.rem(spot, layer_devices),
        )

    def around(mine, count, act):
        if count <= 8:
            for k in range(1, count):
                act(lax.rem(mine + k, count))
        else:

            @pl.loop(1, count)
            def _(k):
                act(lax.rem(mine + k, count))

    def send(src, dst, send_sem, recv_sem, device):
        pltpu.make_async_remote_copy(
            src_ref=src,
            dst_ref=dst,
            send_sem=send_sem,
            recv_sem=recv_sem,
            device_id=device,
            device_id_type=MESH,
        ).start()

    def wait_bytes(ref, sem):
        pltpu.make_async_copy(ref, ref, sem).wait()

    barrier = pltpu.get_barrier_semaphore()

    def greet(device):
        pl.semaphore_signal(barrier, inc=1, device_id=device, device_id_type=MESH)

    around(my_spot, spots, lambda peer: greet(place(my_quad, peer)))
    around(my_quad, quads, lambda peer: greet(place(peer, my_spot)))

    a_copy = pltpu.make_async_copy(a_hbm.at[0, 0], a_ref, a_sem)
    a_copy.start()

    slot_ids = lax.broadcasted_iota(jnp.int32, (slots_p, 1), 0)
    for t in range(local_rows):
        tiles = p_ref[t, 0].astype(jnp.float32)
        ids = jnp.full((slots_p, 1), -1, jnp.int32)
        for s in range(slots_p):
            ids = jnp.where(slot_ids == s, pcols_ref[t, 0, s], ids)
        for panel in range(2):
            picked = jnp.sum(jnp.where(ids == panel, tiles, 0.0), axis=0, keepdims=True)
            for j in range(pairs):
                wf_ref[t, j : j + 1, panel * LANES : (panel + 1) * LANES] = picked[
                    :, j * LANES : (j + 1) * LANES
                ]
    own = wf_ref[...].astype(jnp.bfloat16)
    wb_ref[...] = own
    colw_ref[my_row] = own
    roww_ref[my_spot] = own

    a_copy.wait()
    ids = cols_ref[0] * block_rows + rows_ref[0]
    slot_row = lax.broadcasted_iota(jnp.int32, (1, slot_total), 1)
    ids = jnp.where(slot_row < count_ref[0, 0], ids, -1)
    for c in range(block_cols):
        wanted = c * block_rows + lax.broadcasted_iota(
            jnp.int32, (block_rows, slot_total), 0
        )
        onehot = (ids == wanted).astype(jnp.float32).astype(jnp.bfloat16)
        dense = jnp.dot(onehot, a_ref[...], preferred_element_type=jnp.float32)
        dense = dense.astype(jnp.bfloat16)
        for j in range(pairs):
            lhs_ref[j * block_rows : (j + 1) * block_rows, c * LANES : (c + 1) * LANES] = (
                dense[:, j * LANES : (j + 1) * LANES]
            )

    pl.semaphore_wait(barrier, spots + quads - 2)
    around(
        my_row,
        row_devices,
        lambda peer: send(
            wb_ref,
            colw_ref.at[my_row],
            colw_send,
            colw_recv,
            place(peer * 2 + my_pair, my_spot),
        ),
    )
    around(
        my_spot,
        spots,
        lambda peer: send(
            wb_ref, roww_ref.at[my_spot], roww_send, roww_recv, place(my_quad, peer)
        ),
    )

    wait_bytes(colw_ref.at[pl.ds(0, row_devices - 1)], colw_recv)
    out_row = lax.broadcasted_iota(jnp.int32, (LANES, TILE), 0)
    in_row = lax.broadcasted_iota(jnp.int32, (LANES, TILE), 1)
    parity = out_row // TILE
    inner = out_row % TILE
    spread = jnp.where((inner % 2) == parity, 0, pairs) + inner // 2
    spread = (in_row == spread).astype(jnp.float32).astype(jnp.bfloat16)
    lane = lax.broadcasted_iota(jnp.int32, (LANES, 2 * LANES), 1)
    sub = lax.broadcasted_iota(jnp.int32, (LANES, 2 * LANES), 0)
    keep = ((lane // TILE) % 2) == (sub // TILE)
    for c in range(block_cols):
        block = colw_ref[c // local_rows, c % local_rows].astype(jnp.float32)
        swapped = jnp.concatenate(
            [pltpu.roll(block[:, :LANES], TILE, 1), pltpu.roll(block[:, LANES:], TILE, 1)],
            axis=1,
        )
        both = jnp.concatenate([block, swapped], axis=0).astype(jnp.bfloat16)
        made = jnp.dot(spread, both, preferred_element_type=jnp.float32)
        rhs_ref[c * LANES : (c + 1) * LANES, :] = jnp.where(keep, made, 0.0).astype(
            jnp.bfloat16
        )

    y = jnp.dot(lhs_ref[...], rhs_ref[...], preferred_element_type=jnp.float32)
    for h in range(2):
        y_ref[h] = y[:, h * LANES : (h + 1) * LANES]
    def product_rows(pair, spot, t):
        group = (lax.div(spot, layer_devices) * 2 + pair) * layer_devices + lax.rem(
            spot, layer_devices
        )
        return [
            y_ref[h, pl.ds(t * groups + group, pairs, stride=block_rows), :]
            for h in range(2)
        ]

    for spot in range(spots):
        for t in range(local_rows):
            at = (spot * local_rows + t) * pairs
            for h, rows in enumerate(product_rows(1 - my_pair, spot, t)):
                y2_ref[at : at + pairs, h * LANES : (h + 1) * LANES] = rows.astype(
                    jnp.bfloat16
                )
    sibling = place(my_row * 2 + 1 - my_pair, my_spot)
    send(y2_ref, yrecv_ref, pair_send, pair_recv, sibling)
    wait_bytes(yrecv_ref, pair_recv)
    for spot in range(spots):
        for t in range(local_rows):
            at = (spot * local_rows + t) * pairs
            for h, rows in enumerate(product_rows(my_pair, spot, t)):
                spans = (slice(at, at + pairs), slice(h * LANES, (h + 1) * LANES))
                ysum_ref[spans] = (rows + yrecv_ref[spans].astype(jnp.float32)).astype(
                    jnp.bfloat16
                )

    turned = ysum_ref[...].T
    wait_bytes(roww_ref.at[pl.ds(0, spots - 1)], roww_recv)
    window = roww_ref[...].reshape(spots * local_rows * pairs, 2 * LANES)
    m = jnp.dot(turned, window, preferred_element_type=jnp.float32)

    def fold(i, j):
        top = m[i * LANES : i * LANES + TILE, j * LANES : (j + 1) * LANES]
        low = m[i * LANES + TILE : (i + 1) * LANES, j * LANES : (j + 1) * LANES]
        return top + pltpu.roll(low, TILE, 1)

    left = lax.broadcasted_iota(jnp.int32, (TILE // 2, LANES), 1) < TILE
    upper = jnp.concatenate([fold(0, 0), fold(1, 0)], axis=0).T[:TILE]
    corner = fold(1, 1)
    corner = jnp.concatenate([corner, corner], axis=0).T[:TILE]
    lower = jnp.where(left, corner[: TILE // 2], corner[TILE // 2 :])
    packed = [upper, lower]
    spare = part_ref.shape[0] * part_ref.shape[1] - TILE - TILE // 2
    if spare:
        packed.append(jnp.zeros((spare, LANES), jnp.float32))
    part_ref[...] = jnp.concatenate(packed, axis=0).reshape(part_ref.shape)

    around(
        my_quad,
        quads,
        lambda peer: send(
            part_ref.at[peer],
            first_ref.at[my_quad],
            first_send,
            first_recv,
            place(peer, my_spot),
        ),
    )
    first_ref[my_quad] = part_ref[my_quad]
    wait_bytes(first_ref.at[pl.ds(0, quads - 1)], first_recv)
    second_ref[my_spot] = jnp.sum(first_ref[...], axis=0)
    around(
        my_spot,
        spots,
        lambda peer: send(
            second_ref.at[my_spot],
            second_ref.at[my_spot],
            second_send,
            second_recv,
            place(my_quad, peer),
        ),
    )
    wait_bytes(second_ref.at[pl.ds(0, spots - 1)], second_recv)
    third_ref[my_quad] = jnp.sum(second_ref[...], axis=0)
    around(
        my_quad,
        quads,
        lambda peer: send(
            third_ref.at[my_quad],
            third_ref.at[my_quad],
            third_send,
            third_recv,
            place(peer, my_spot),
        ),
    )
    wait_bytes(third_ref.at[pl.ds(0, quads - 1)], third_recv)

    summed = third_ref[...].reshape(-1, LANES)
    out_ref[:, :LANES] = summed[:TILE]
    corner = summed[TILE : TILE + TILE // 2]
    out_ref[: TILE // 2, LANES:] = corner[:, :TILE]
    out_ref[TILE // 2 :, LANES:] = pltpu.roll(corner, TILE, 1)[:, :TILE]
    wait_bytes(colw_ref.at[pl.ds(0, row_devices - 1)], colw_send)
    wait_bytes(roww_ref.at[pl.ds(0, spots - 1)], roww_send)
    wait_bytes(y2_ref, pair_send)
    wait_bytes(first_ref.at[pl.ds(0, quads - 1)], first_send)
    wait_bytes(second_ref.at[pl.ds(0, spots - 1)], second_send)
    wait_bytes(third_ref.at[pl.ds(0, quads - 1)], third_send)


def per_device(a_tiles, a_rows, a_cols, a_count, p_tiles, p_cols):
    row_devices = lax.axis_size("row")
    col_devices = lax.axis_size("col")
    layer_devices = lax.axis_size("layer")
    groups = col_devices * layer_devices
    spots = groups // 2
    quads = 2 * row_devices
    local_rows = p_tiles.shape[0]
    slot_total = a_tiles.shape[2]
    pairs = TILE // 2
    block_rows = local_rows * groups
    block_cols = local_rows * row_devices
    packed_rows = TILE + TILE // 2
    chunk = pl.cdiv(pl.cdiv(packed_rows, quads), CHUNK) * CHUNK
    half_rows = spots * local_rows * pairs
    sizes = (row_devices, col_devices, layer_devices)
    vmem = pl.BlockSpec(memory_space=pltpu.VMEM)
    smem = pl.BlockSpec(memory_space=pltpu.SMEM)
    wide = 2 * LANES
    return pl.pallas_call(
        functools.partial(kernel, sizes),
        out_shape=pltpu.VMEM((PB * TILE, 3 * PB * TILE), jnp.float32),
        in_specs=[pl.BlockSpec(memory_space=pl.ANY), vmem, vmem, smem, vmem, smem],
        out_specs=vmem,
        scratch_shapes=[
            pltpu.VMEM((slot_total, TILE * TILE), jnp.bfloat16),
            pltpu.VMEM((local_rows, pairs, wide), jnp.float32),
            pltpu.VMEM((local_rows, pairs, wide), jnp.bfloat16),
            pltpu.VMEM((row_devices, local_rows, pairs, wide), jnp.bfloat16),
            pltpu.VMEM((spots, local_rows, pairs, wide), jnp.bfloat16),
            pltpu.VMEM((pairs * block_rows, block_cols * LANES), jnp.bfloat16),
            pltpu.VMEM((block_cols * LANES, wide), jnp.bfloat16),
            pltpu.VMEM((2, pairs * block_rows, LANES), jnp.float32),
            pltpu.VMEM((half_rows, wide), jnp.bfloat16),
            pltpu.VMEM((half_rows, wide), jnp.bfloat16),
            pltpu.VMEM((half_rows, wide), jnp.bfloat16),
            pltpu.VMEM((quads, chunk, LANES), jnp.float32),
            pltpu.VMEM((quads, chunk, LANES), jnp.float32),
            pltpu.VMEM((spots, chunk, LANES), jnp.float32),
            pltpu.VMEM((quads, chunk, LANES), jnp.float32),
        ]
        + [pltpu.SemaphoreType.DMA] * 13,
        compiler_params=pltpu.CompilerParams(
            collective_id=0, has_side_effects=True, vmem_limit_bytes=56 << 20
        ),
    )(a_tiles, a_rows, a_cols, a_count, p_tiles, p_cols)


def solution(mesh):
    placed = (
        P("row", ("col", "layer"), None, None),
        P("row", ("col", "layer"), None),
        P("row", ("col", "layer"), None),
        P("row", ("col", "layer")),
        P("row", ("col", "layer"), None, None),
        P("row", ("col", "layer"), None),
    )
    return jax.shard_map(per_device, mesh=mesh, in_specs=placed, out_specs=P(), check_vma=False)
```
